512 devices in a mesh: dp: 64 (over y_lo, z, core), node: 8 (over x, y_hi).
Axes of the slice: x: 4, y: 8 (y_hi: 2, y_lo: 4; y = y_hi * 4 + y_lo), z: 8, core: 2. Of those that a mesh axis runs over, the one named last changes fastest.
Arguments:
- tokens: bfloat16 [1024, 4096], P('dp', 'node'), may hold values from -200 to 200
- cotangent: bfloat16 [1024, 4096], P('dp', 'node'), may hold values from -6 to 6
- norm_gain: float32 [4096], P('node'), may hold values from 0.1 to 1.9
- gate_weight: bfloat16 [10240, 4096], P('dp', 'node'), may hold values from -0.09375 to 0.09375
- up_weight: bfloat16 [10240, 4096], P('dp', 'node'), may hold values from -0.09375 to 0.09375
- down_weight: bfloat16 [10240, 4096], P('dp', 'node'), may hold values from -0.0625 to 0.0625
Outputs:
- branch_out: bfloat16 [1024, 4096], P('dp', 'node')
- grad_tokens: bfloat16 [1024, 4096], P('dp', 'node')
- grad_gate_weight: float32 [10240, 4096], P('dp', 'node')
- grad_up_weight: float32 [10240, 4096], P('dp', 'node')
- grad_down_weight: float32 [10240, 4096], P('dp', 'node')
- grad_norm_gain: float32 [4096], P('node')
The draws below stay inside these ranges and needn't reach their ends.
All inputs are finite; a program needn't handle non-finite values.
Results may differ from the reference program's by a relative error of at most 0.0065.
Values may be sent and summed in bfloat16 or wider, within the bound.
A program may use at most 64 MiB of HBM per device.

```python
import math
import jax
import jax.numpy as jnp
from jax import lax

D = 4096
FF = 10240
TOK = 1024


def draw_tokens(key, part):
    key = jax.random.fold_in(key, 11)
    first, second, third = jax.random.split(key, 3)
    position = jnp.arange(D, dtype=jnp.float32) / (D - 1)
    base = jnp.clip(jax.random.normal(first, (TOK, D), jnp.float32), -6.0, 6.0)
    column_power = 0.5 * position + 0.5 * jax.random.uniform(second, (D,), jnp.float32)
    row_power = 0.5 * jax.random.uniform(third, (TOK, 1), jnp.float32, -1.0, 1.0)
    values = base * jnp.power(10.0, column_power)[None, :] * jnp.power(10.0, row_power)
    return values.astype(jnp.bfloat16)


def block_scale(rng, shape, shards, smallest, top_value):
    gain = 1.0
    for dim, parts in shards:
        steps = jax.random.uniform(jax.random.fold_in(jax.random.fold_in(rng, 6), dim), (parts,), jnp.float32, smallest / len(shards), top_value / len(shards))
        gain = gain * jnp.repeat(jnp.exp(steps), shape[dim] // parts).reshape((-1,) + (1,) * (len(shape) - 1 - dim))
    return gain


def noise(key, dims, deviation, reach, cuts=(), kind=jnp.bfloat16):
    result = deviation * jax.random.normal(key, dims, jnp.float32)
    if cuts:
        result = result * block_scale(key, dims, cuts, -0.22, 0.18)
    return jnp.clip(result, -reach, reach).astype(kind)


def setup_inputs(seed: int = 0) -> dict:
    keys = jax.random.split(jax.random.key(seed), 7)
    return {
        "tokens": draw_tokens(jax.random.fold_in(keys[6], 71), 0),
        "cotangent": noise(keys[1], (TOK, D), 1.0, 6.0, ((0, 64), (1, 8))),
        "norm_gain": jnp.clip(1.0 + 0.18 * jax.random.normal(keys[2], (D,), jnp.float32), 0.1, 1.9),
        "gate_weight": noise(keys[3], (FF, D), D ** -0.5, 0.09375, ((0, 64), (1, 8))),
        "up_weight": noise(keys[4], (FF, D), D ** -0.5, 0.09375, ((0, 64), (1, 8))),
        "down_weight": noise(keys[5], (FF, D), FF ** -0.5, 0.0625, ((0, 64), (1, 8))),
    }


EPSILON = 1e-06
GELU_SCALE = math.sqrt(2.0 / math.pi)

def gelu_parts(value):
    inner = GELU_SCALE * (value + 0.044715 * value * value * value)
    tanh_inner = jnp.tanh(inner)
    activated = 0.5 * value * (1.0 + tanh_inner)
    slope = 0.5 * (1.0 + tanh_inner) + 0.5 * value * (1.0 - tanh_inner * tanh_inner) * GELU_SCALE * (1.0 + 3.0 * 0.044715 * value * value)
    return (activated, slope)

def reference(tokens, cotangent, norm_gain, gate_weight, up_weight, down_weight):
    widened = tokens.astype(jnp.float32)
    mean_square = lax.optimization_barrier(jnp.mean(widened * widened, axis=1))
    inv_rms = lax.rsqrt(mean_square + EPSILON)
    scaled = widened * inv_rms[:, None]
    normed = (scaled * norm_gain).astype(jnp.bfloat16)
    gate_value = jnp.dot(gate_weight, normed.T, preferred_element_type=jnp.float32)
    up_value = jnp.dot(up_weight, normed.T, preferred_element_type=jnp.float32)
    activated, slope = gelu_parts(gate_value)
    hidden = (activated * up_value).astype(jnp.bfloat16)
    branch_out = jnp.dot(hidden.T, down_weight, preferred_element_type=jnp.float32).astype(jnp.bfloat16)
    back_hidden = jnp.dot(down_weight, cotangent.T, preferred_element_type=jnp.float32)
    grad_gate = (back_hidden * up_value * slope).astype(jnp.bfloat16)
    grad_up = (back_hidden * activated).astype(jnp.bfloat16)
    grad_down_weight = jnp.dot(hidden, cotangent, preferred_element_type=jnp.float32)
    grad_gate_weight = jnp.dot(grad_gate, normed, preferred_element_type=jnp.float32)
    grad_up_weight = jnp.dot(grad_up, normed, preferred_element_type=jnp.float32)
    grad_normed = jnp.dot(grad_gate.T, gate_weight, preferred_element_type=jnp.float32) + jnp.dot(grad_up.T, up_weight, preferred_element_type=jnp.float32)
    grad_norm_gain = lax.optimization_barrier(jnp.sum(grad_normed * scaled, axis=0))
    grad_scaled = grad_normed * norm_gain
    row_mean = lax.optimization_barrier(jnp.mean(grad_scaled * scaled, axis=1))
    grad_tokens = (inv_rms[:, None] * (grad_scaled - scaled * row_mean[:, None])).astype(jnp.bfloat16)
    return (branch_out, grad_tokens, grad_gate_weight, grad_up_weight, grad_down_weight, grad_norm_gain)
```

```python
import functools
import math

import jax
import jax.numpy as jnp
from jax import lax
from jax.experimental import pallas as pl
from jax.experimental.pallas import tpu as pltpu
from jax.sharding import PartitionSpec as P

D = 4096
EPSILON = 1e-06
GELU_SCALE = math.sqrt(2.0 / math.pi)
MESH = pl.DeviceIdType.MESH
F32 = jnp.float32
BF16 = jnp.bfloat16

GROUPS = ((0, 1), (1, 3), (3, 5), (5, 7), (7, 8))
UNITS = 160
NT = (((1,), (1,)), ((), ()))
TN = (((0,), (0,)), ((), ()))


def dot(a, b, dims=None):
    if dims is None:
        return jnp.dot(a, b, preferred_element_type=F32)
    return lax.dot_general(a, b, dims, preferred_element_type=F32)


def gelu_parts(value):
    inner = GELU_SCALE * (value + 0.044715 * value * value * value)
    tanh_inner = jnp.tanh(inner)
    activated = 0.5 * value * (1.0 + tanh_inner)
    slope = 0.5 * (1.0 + tanh_inner) + 0.5 * value * (
        1.0 - tanh_inner * tanh_inner
    ) * GELU_SCALE * (1.0 + 3.0 * 0.044715 * value * value)
    return (activated, slope)


def pair(value):
    high = value.astype(BF16).astype(F32)
    return high, (value - high).astype(BF16).astype(F32)


def put(wide, lane, *values):
    at = lax.broadcasted_iota(jnp.int32, wide.shape, 1)
    for i, value in enumerate(values):
        wide = jnp.where(at == lane + i, value, wide)
    return wide


class Copies:
    def __init__(self, send_sem, recv_sem):
        self.send_sem, self.recv_sem, self.count, self.all = send_sem, recv_sem, 0, []

    def __call__(self, src, dst, device):
        i = self.count
        self.count += 1
        copy = pltpu.make_async_remote_copy(
            src_ref=src,
            dst_ref=dst,
            send_sem=self.send_sem.at[i],
            recv_sem=self.recv_sem.at[i],
            device_id=device,
            device_id_type=MESH,
        )
        copy.start()
        self.all.append(copy)
        return copy


N_COPIES = 120


def kernel(
    tok_hbm, cot_hbm, gain_hbm, gate_hbm, up_hbm, down_hbm,
    branch_hbm, gtok_hbm, dgate_hbm, dup_hbm, ddown_hbm, dgain_hbm,
    own_tok, gain_v, tok, cot, w, w_high, w_low, wd, part, part_own, rx, y_out, y_in, hid,
    normed, branch_part, gn_part, ring_b, ring_g, ring_b_out, ring_g_out,
    last_b, last_g, last_b_out, last_g_out, last_b_in, last_g_in,
    dw, dd, dw_in, dgain, dgain_in, dgain_y, dgain_y_in, dgain_c, dgain_c_in,
    o_branch, o_gtok, o_dgain,
    send_sem, recv_sem, local_sem,
):
    dp, node = lax.axis_index("dp"), lax.axis_index("node")
    x, yh = node // 2, node % 2
    yl, z, c = dp // 16, (dp // 2) % 8, dp % 2

    def at(dx=0, dyh=0, dyl=0, dz=0, dc=0):
        return (
            lax.rem(yl + dyl, 4) * 16 + lax.rem(z + dz, 8) * 2 + lax.rem(c + dc, 2),
            lax.rem(x + dx, 4) * 2 + lax.rem(yh + dyh, 2),
        )

    sibling, across = at(dc=1), at(dyh=1)
    ahead, behind = at(dz=1), at(dz=7)

    def piece(k):
        return lax.rem(k - x + 8, 4)

    local = []

    def bring(src, dst):
        copy = pltpu.make_async_copy(src, dst, local_sem.at[len(local)])
        copy.start()
        local.append(copy)
        return copy

    mine = piece(0)
    b_tok = bring(tok_hbm, tok.at[0, mine])
    b_cot = bring(cot_hbm, cot.at[0, mine])
    b_own = bring(tok_hbm, own_tok)
    b_gain = bring(gain_hbm, gain_v)
    b_gate = bring(gate_hbm, w.at[pl.ds(0, UNITS)])
    b_up = bring(up_hbm, w.at[pl.ds(2 * UNITS, UNITS)])
    b_down = bring(down_hbm, wd.at[pl.ds(0, UNITS)])

    barrier = pltpu.get_barrier_semaphore()
    partners = [sibling, across]
    partners += [at(dx=k) for k in (1, 2, 3)]
    partners += [at(dyl=k) for k in (1, 2, 3)]
    partners += [at(dz=k) for k in range(1, 8)]
    for device in partners:
        pl.semaphore_signal(barrier, 1, device_id=device, device_id_type=MESH)
    wd[pl.ds(2 * UNITS, 64)] = jnp.zeros((64, 512), BF16)
    pl.semaphore_wait(barrier, len(partners))

    remote = Copies(send_sem, recv_sem)

    y_tok = [remote(tok_hbm, tok.at[0, piece(4 - k)], at(dyl=k)) for k in (1, 2, 3)]
    y_cot = [remote(cot_hbm, cot.at[0, piece(4 - k)], at(dyl=k)) for k in (1, 2, 3)]
    s_gate = remote(gate_hbm, w.at[pl.ds(UNITS, UNITS)], sibling)
    s_up = remote(up_hbm, w.at[pl.ds(3 * UNITS, UNITS)], sibling)
    s_down = remote(down_hbm, wd.at[pl.ds(UNITS, UNITS)], sibling)

    def fold(block):
        rows = pl.ds(block * UNITS, UNITS)
        high, low = pair(w[rows].astype(F32) * gain_v[...])
        w_high[rows] = high.astype(BF16)
        w_low[rows] = low.astype(BF16)

    b_gain.wait()
    b_gate.wait()
    fold(0)
    b_up.wait()
    fold(2)
    b_tok.wait()
    b_cot.wait()
    b_down.wait()
    b_own.wait()

    def ring(buffer, step, both, way):
        copies = []
        if both or way > 0:
            src = 0 if step == 1 else 2 * (step - 1)
            copies.append(remote(buffer.at[src], buffer.at[min(2 * step, 7)], ahead))
        if both or way < 0:
            src = 0 if step == 1 else 2 * (step - 1) - 1
            copies.append(remote(buffer.at[src], buffer.at[2 * step - 1], behind))
        return copies

    for copy in y_tok:
        copy.wait_recv()
    r_tok = ring(tok, 1, True, 0)
    for copy in y_cot:
        copy.wait_recv()
    r_cot = ring(cot, 1, True, 0)

    s_gate.wait_recv()
    fold(1)
    s_up.wait_recv()
    fold(3)
    s_down.wait_recv()

    def multiply(g):
        a, b = GROUPS[g]
        n = b - a
        t = tok[a:b].reshape(n * 64, 512)
        gate_up = dot(t, w_high[...], NT) + dot(t, w_low[...], NT)
        back = dot(cot[a:b].reshape(n * 64, 512), wd[...], NT)
        wide = t.astype(F32)
        back = put(back, 2 * UNITS, *pair(jnp.sum(wide * wide, axis=1, keepdims=True)))
        gate_up = gate_up.reshape(n, 4, 16, 4 * UNITS)
        back = back.reshape(n, 4, 16, 384)
        part[a:b, :, :, 0:640] = gate_up.astype(BF16)
        part[a:b, :, :, 640:1024] = back.astype(BF16)
        part_own[a:b, :, 0:640] = gate_up[:, 0]
        part_own[a:b, :, 640:1024] = back[:, 0]
        return [
            remote(part.at[pl.ds(a, n), k], rx.at[k - 1, pl.ds(a, n)], at(dx=k))
            for k in (1, 2, 3)
        ]

    def add_x(g, copies):
        a, b = GROUPS[g]
        n = b - a
        for copy in copies:
            copy.wait_recv()
        total = part_own[a:b]
        for k in range(3):
            total = total + rx[k, a:b].astype(F32)
        part_own[a:b] = total
        total = total.reshape(n * 16, 1024)
        squares = total[:, 960:961] + total[:, 961:962]
        y_out[a:b, :, 0:640] = total[:, 0:640].astype(BF16).reshape(n, 16, 640)
        last = put(total[:, 640:1024], 320, *pair(squares))
        y_out[a:b, :, 640:1024] = last.astype(BF16).reshape(n, 16, 384)
        return remote(y_out.at[pl.ds(a, n)], y_in.at[pl.ds(a, n)], across)

    x_sent, y_sent = [], []
    x_sent.append(multiply(0))
    for step in (1, 2, 3, 4):
        for copy in r_tok:
            copy.wait_recv()
        if step < 4:
            r_tok = ring(tok, step + 1, step < 3, -1)
        for copy in r_cot:
            copy.wait_recv()
        if step < 4:
            r_cot = ring(cot, step + 1, step < 3, 1)
        x_sent.append(multiply(step))
        y_sent.append(add_x(step - 1, x_sent[step - 1]))
    y_sent.append(add_x(4, x_sent[4]))

    def pointwise(g):
        a, b = GROUPS[g]
        n = b - a
        y_sent[g].wait_recv()
        total = (part_own[a:b] + y_in[a:b].astype(F32)).reshape(n * 16, 1024)
        squares = total[:, 960:961] + total[:, 961:962]
        inv_rms = lax.rsqrt(squares / D + EPSILON)
        gate_value = total[:, 0:320] * inv_rms
        up_value = total[:, 320:640] * inv_rms
        last = total[:, 640:1024]
        back = last[:, 0:320]
        activated, slope = gelu_parts(gate_value)
        grad_gate = (back * up_value * slope).astype(BF16)
        grad_up = (back * activated).astype(BF16)
        along = jnp.sum(
            grad_gate.astype(F32) * gate_value + grad_up.astype(F32) * up_value,
            axis=1,
            keepdims=True,
        )
        hid[a:b, 0, :, 0:640] = jnp.concatenate([grad_gate, grad_up], axis=1).reshape(n, 16, 640)
        hidden = jnp.concatenate([activated * up_value, jnp.zeros((n * 16, 64), F32)], axis=1)
        hidden = put(hidden, 320, *pair(along), *pair(inv_rms))
        hid[a:b, 0, :, 640:1024] = hidden.astype(BF16).reshape(n, 16, 384)
        return [
            remote(hid.at[pl.ds(a, n), 0], hid.at[pl.ds(a, n), 4 - k], at(dx=k))
            for k in (1, 2, 3)
        ]

    h_sent = {g: pointwise(g) for g in (0, 1, 4, 3, 2)}

    def inverse(block):
        return block[:, 962:963].astype(F32) + block[:, 963:964].astype(F32)

    def terms(g, gain_sum):
        a, b = GROUPS[g]
        n = b - a
        for copy in h_sent[g]:
            copy.wait_recv()
        block = hid[a:b].reshape(n * 64, 1024)
        branch_part[a:b] = dot(block[:, 640:1024], wd[...]).reshape(n, 64, 512)
        grad = dot(block[:, 0:640], w[...])
        scaled = tok[a:b].reshape(n * 64, 512).astype(F32) * inverse(block)
        normed[a:b] = (scaled * gain_v[...]).astype(BF16).reshape(n, 64, 512)
        gain_sum = gain_sum + jnp.sum(grad * scaled, axis=0, keepdims=True)
        gn_part[a:b, :, 0:512] = grad.reshape(n, 64, 512)
        along = block[:, 960:961].astype(F32) + block[:, 961:962].astype(F32)
        extra = put(jnp.zeros((n * 64, 128), F32), 0, along)
        gn_part[a:b, :, 512:640] = extra.reshape(n, 64, 128)
        return gain_sum

    def rounded(total):
        along = total[:, 512:513] + total[:, 513:514]
        return jnp.concatenate(
            [total[:, 0:512].astype(BF16), put(total[:, 512:640], 0, *pair(along)).astype(BF16)],
            axis=1,
        )

    gain_sum = jnp.zeros((1, 512), F32)
    gain_sum = terms(4, gain_sum)
    ring_b_out[0, 0] = branch_part[7].astype(BF16)
    ring_g_out[0, 1] = rounded(gn_part[7])
    arrived_b = {0: remote(ring_b_out.at[0, 0], ring_b.at[0, 0], ahead)}
    arrived_g = {1: remote(ring_g_out.at[0, 1], ring_g.at[0, 1], behind)}
    for step in (2, 3, 4):
        distance = 5 - step
        gain_sum = terms(distance, gain_sum)
        next_b, next_g = {}, {}
        for way in (0, 1):
            slot = 2 * distance - 1 + way
            there = (ahead, behind)[way]
            total = branch_part[slot]
            if way in arrived_b:
                arrived_b[way].wait_recv()
                total = total + ring_b[step - 2, way].astype(F32)
            ring_b_out[step - 1, way] = total.astype(BF16)
            next_b[way] = remote(ring_b_out.at[step - 1, way], ring_b.at[step - 1, way], there)
        for way in (0, 1):
            slot = 2 * distance - 1 + way
            there = (ahead, behind)[way]
            total = gn_part[slot]
            if way in arrived_g:
                arrived_g[way].wait_recv()
                total = total + ring_g[step - 2, way].astype(F32)
            ring_g_out[step - 1, way] = rounded(total)
            next_g[way] = remote(ring_g_out.at[step - 1, way], ring_g.at[step - 1, way], there)
        arrived_b, arrived_g = next_b, next_g

    gain_sum = terms(0, gain_sum)
    dgain[...] = jnp.broadcast_to(gain_sum, (8, 512))
    z_gain = [remote(dgain, dgain_in.at[k - 1], at(dz=k)) for k in range(1, 8)]

    every = hid[...].reshape(512, 1024)
    dw[...] = dot(every[:, 0:640], normed[...].reshape(512, 512), TN)
    dd[...] = dot(every[:, 640:1024], cot[...].reshape(512, 512), TN)
    w_sent = [
        remote(dw.at[pl.ds(UNITS, UNITS)], dw_in.at[0], sibling),
        remote(dw.at[pl.ds(3 * UNITS, UNITS)], dw_in.at[1], sibling),
        remote(dd.at[pl.ds(UNITS, UNITS)], dw_in.at[2], sibling),
    ]

    for copy in arrived_b.values():
        copy.wait_recv()
    total = branch_part[0] + ring_b[3, 0].astype(F32) + ring_b[3, 1].astype(F32)
    last_b[...] = total.reshape(4, 16, 512)
    last_b_out[...] = total.astype(BF16).reshape(4, 16, 512)
    y_b = [remote(last_b_out.at[piece(k)], last_b_in.at[k - 1], at(dyl=k)) for k in (1, 2, 3)]
    for copy in arrived_g.values():
        copy.wait_recv()
    total = gn_part[0] + ring_g[3, 0].astype(F32) + ring_g[3, 1].astype(F32)
    last_g[...] = total.reshape(4, 16, 640)
    last_g_out[...] = rounded(total).reshape(4, 16, 640)
    y_g = [remote(last_g_out.at[piece(k)], last_g_in.at[k - 1], at(dyl=k)) for k in (1, 2, 3)]

    for copy in z_gain:
        copy.wait_recv()
    total = dgain[...]
    for k in range(7):
        total = total + dgain_in[k]
    dgain_y[...] = total
    g_y = [remote(dgain_y, dgain_y_in.at[k - 1], at(dyl=k)) for k in (1, 2, 3)]

    for i, (grad, row, out) in enumerate(((dw, 0, dgate_hbm), (dw, 2 * UNITS, dup_hbm), (dd, 0, ddown_hbm))):
        w_sent[i].wait_recv()
        rows = pl.ds(row, UNITS)
        grad[rows] = grad[rows] + dw_in[i]
        bring(grad.at[rows], out)

    for copy in y_b:
        copy.wait_recv()
    total = last_b[mine]
    for k in range(3):
        total = total + last_b_in[k].astype(F32)
    o_branch[...] = total.astype(BF16)
    bring(o_branch, branch_hbm)

    for copy in g_y:
        copy.wait_recv()
    total = dgain_y[...]
    for k in range(3):
        total = total + dgain_y_in[k]
    dgain_c[...] = total
    g_c = remote(dgain_c, dgain_c_in, sibling)

    for copy in y_g:
        copy.wait_recv()
    total = last_g[mine]
    for k in range(3):
        total = total + last_g_in[k].astype(F32)
    row_mean = (total[:, 512:513] + total[:, 513:514]) / D
    inv_rms = inverse(hid[0, mine])
    scaled = own_tok[...].astype(F32) * inv_rms
    o_gtok[...] = (inv_rms * (total[:, 0:512] * gain_v[...] - scaled * row_mean)).astype(BF16)
    bring(o_gtok, gtok_hbm)

    g_c.wait_recv()
    o_dgain[...] = (dgain_c[...] + dgain_c_in[...])[0:1]
    bring(o_dgain, dgain_hbm)

    for copy in remote.all:
        copy.wait_send()
    for copy in local[7:]:
        copy.wait()


def on_device(tokens, cotangent, norm_gain, gate_weight, up_weight, down_weight):
    vmem, dma = pltpu.VMEM, pltpu.SemaphoreType.DMA
    grad = jax.ShapeDtypeStruct((UNITS, 512), F32)
    outs = pl.pallas_call(
        kernel,
        out_shape=(
            jax.ShapeDtypeStruct((16, 512), BF16),
            jax.ShapeDtypeStruct((16, 512), BF16),
            grad,
            grad,
            grad,
            jax.ShapeDtypeStruct((1, 512), F32),
        ),
        in_specs=[pl.BlockSpec(memory_space=pl.ANY)] * 6,
        out_specs=[pl.BlockSpec(memory_space=pl.ANY)] * 6,
        scratch_shapes=[
            vmem((16, 512), BF16),
            vmem((1, 512), F32),
            vmem((8, 4, 16, 512), BF16),
            vmem((8, 4, 16, 512), BF16),
            vmem((4 * UNITS, 512), BF16),
            vmem((4 * UNITS, 512), BF16),
            vmem((4 * UNITS, 512), BF16),
            vmem((384, 512), BF16),
            vmem((8, 4, 16, 1024), BF16),
            vmem((8, 16, 1024), F32),
            vmem((3, 8, 16, 1024), BF16),
            vmem((8, 16, 1024), BF16),
            vmem((8, 16, 1024), BF16),
            vmem((8, 4, 16, 1024), BF16),
            vmem((8, 64, 512), BF16),
            vmem((8, 64, 512), F32),
            vmem((8, 64, 640), F32),
            vmem((4, 2, 64, 512), BF16),
            vmem((4, 2, 64, 640), BF16),
            vmem((4, 2, 64, 512), BF16),
            vmem((4, 2, 64, 640), BF16),
            vmem((4, 16, 512), F32),
            vmem((4, 16, 640), F32),
            vmem((4, 16, 512), BF16),
            vmem((4, 16, 640), BF16),
            vmem((3, 16, 512), BF16),
            vmem((3, 16, 640), BF16),
            vmem((4 * UNITS, 512), F32),
            vmem((384, 512), F32),
            vmem((3, UNITS, 512), F32),
            vmem((8, 512), F32),
            vmem((7, 8, 512), F32),
            vmem((8, 512), F32),
            vmem((3, 8, 512), F32),
            vmem((8, 512), F32),
            vmem((8, 512), F32),
            vmem((16, 512), BF16),
            vmem((16, 512), BF16),
            vmem((1, 512), F32),
            dma((N_COPIES,)),
            dma((N_COPIES,)),
            dma((16,)),
        ],
        compiler_params=pltpu.CompilerParams(
            collective_id=0, has_side_effects=True, vmem_limit_bytes=48 * 1024 * 1024
        ),
        cost_estimate=pl.CostEstimate(flops=1_600_000_000, bytes_accessed=1_600_000, transcendentals=50_000),
    )(tokens, cotangent, norm_gain.reshape(1, 512), gate_weight, up_weight, down_weight)
    return (*outs[:5], outs[5].reshape(512))


def solution(mesh):
    split = P("dp", "node")
    return jax.shard_map(
        on_device,
        mesh=mesh,
        in_specs=(split, split, P("node"), split, split, split),
        out_specs=(split, split, split, split, split, P("node")),
        check_vma=False,
    )
```

```python
import functools
import math

import jax
import jax.numpy as jnp
from jax import lax
from jax.experimental import pallas as pl
from jax.experimental.pallas import tpu as pltpu
from jax.sharding import PartitionSpec as P

D = 4096
EPSILON = 1e-06
GELU_SCALE = math.sqrt(2.0 / math.pi)
MESH = pl.DeviceIdType.MESH
F32 = jnp.float32
BF16 = jnp.bfloat16

GROUPS = ((0, 1), (1, 3), (3, 5), (5, 7), (7, 8))
UNITS = 160
NT = (((1,), (1,)), ((), ()))
TN = (((0,), (0,)), ((), ()))


def dot(a, b, dims=None):
    if dims is None:
        return jnp.dot(a, b, preferred_element_type=F32)
    return lax.dot_general(a, b, dims, preferred_element_type=F32)


def gelu_parts(value):
    inner = GELU_SCALE * (value + 0.044715 * value * value * value)
    tanh_inner = jnp.tanh(inner)
    activated = 0.5 * value * (1.0 + tanh_inner)
    slope = 0.5 * (1.0 + tanh_inner) + 0.5 * value * (
        1.0 - tanh_inner * tanh_inner
    ) * GELU_SCALE * (1.0 + 3.0 * 0.044715 * value * value)
    return (activated, slope)


def pair(value):
    high = value.astype(BF16).astype(F32)
    return high, (value - high).astype(BF16).astype(F32)


def put(wide, lane, *values):
    at = lax.broadcasted_iota(jnp.int32, wide.shape, 1)
    for i, value in enumerate(values):
        wide = jnp.where(at == lane + i, value, wide)
    return wide


class Copies:
    def __init__(self, send_sem, recv_sem):
        self.send_sem, self.recv_sem, self.count, self.all = send_sem, recv_sem, 0, []

    def __call__(self, src, dst, device):
        i = self.count
        self.count += 1
        copy = pltpu.make_async_remote_copy(
            src_ref=src,
            dst_ref=dst,
            send_sem=self.send_sem.at[i],
            recv_sem=self.recv_sem.at[i],
            device_id=device,
            device_id_type=MESH,
        )
        copy.start()
        self.all.append(copy)
        return copy


N_COPIES = 120


def kernel(
    tok_hbm, cot_hbm, gain_hbm, gate_hbm, up_hbm, down_hbm,
    branch_hbm, gtok_hbm, dgate_hbm, dup_hbm, ddown_hbm, dgain_hbm,
    own_tok, gain_v, tok, cot, w, w_high, w_low, wd, part, part_own, rx, y_out, y_in, hid,
    normed, branch_part, gn_part, ring_b, ring_g, ring_b_out, ring_g_out,
    last_b, last_g, last_b_out, last_g_out, last_b_in, last_g_in,
    dw, dd, dw_in, dgain, dgain_in, dgain_y, dgain_y_in, dgain_c, dgain_c_in,
    o_branch, o_gtok, o_dgain,
    send_sem, recv_sem, local_sem,
):
    dp, node = lax.axis_index("dp"), lax.axis_index("node")
    x, yh = node // 2, node % 2
    yl, z, c = dp // 16, (dp // 2) % 8, dp % 2

    def at(dx=0, dyh=0, dyl=0, dz=0, dc=0):
        return (
            lax.rem(yl + dyl, 4) * 16 + lax.rem(z + dz, 8) * 2 + lax.rem(c + dc, 2),
            lax.rem(x + dx, 4) * 2 + lax.rem(yh + dyh, 2),
        )

    sibling, across = at(dc=1), at(dyh=1)
    ahead, behind = at(dz=1), at(dz=7)

    def piece(k):
        return lax.rem(k - x + 8, 4)

    local = []

    def bring(src, dst):
        copy = pltpu.make_async_copy(src, dst, local_sem.at[len(local)])
        copy.start()
        local.append(copy)
        return copy

    mine = piece(0)
    b_tok = bring(tok_hbm, tok.at[0, mine])
    b_cot = bring(cot_hbm, cot.at[0, mine])
    b_own = bring(tok_hbm, own_tok)
    b_gain = bring(gain_hbm, gain_v)
    b_gate = bring(gate_hbm, w.at[pl.ds(0, UNITS)])
    b_up = bring(up_hbm, w.at[pl.ds(2 * UNITS, UNITS)])
    b_down = bring(down_hbm, wd.at[pl.ds(0, UNITS)])

    barrier = pltpu.get_barrier_semaphore()
    partners = [sibling, across]
    partners += [at(dx=k) for k in (1, 2, 3)]
    partners += [at(dyl=k) for k in (1, 2, 3)]
    partners += [at(dz=k) for k in range(1, 8)]
    for device in partners:
        pl.semaphore_signal(barrier, 1, device_id=device, device_id_type=MESH)
    wd[pl.ds(2 * UNITS, 64)] = jnp.zeros((64, 512), BF16)
    pl.semaphore_wait(barrier, len(partners))

    remote = Copies(send_sem, recv_sem)

    y_tok = [remote(tok_hbm, tok.at[0, piece(4 - k)], at(dyl=k)) for k in (1, 2, 3)]
    y_cot = [remote(cot_hbm, cot.at[0, piece(4 - k)], at(dyl=k)) for k in (1, 2, 3)]
    s_gate = remote(gate_hbm, w.at[pl.ds(UNITS, UNITS)], sibling)
    s_up = remote(up_hbm, w.at[pl.ds(3 * UNITS, UNITS)], sibling)
    s_down = remote(down_hbm, wd.at[pl.ds(UNITS, UNITS)], sibling)

    def fold(block):
        rows = pl.ds(block * UNITS, UNITS)
        high, low = pair(w[rows].astype(F32) * gain_v[...])
        w_high[rows] = high.astype(BF16)
        w_low[rows] = low.astype(BF16)

    b_gain.wait()
    b_gate.wait()
    fold(0)
    b_up.wait()
    fold(2)
    b_tok.wait()
    b_cot.wait()
    b_down.wait()
    b_own.wait()

    def ring(buffer, step, both, way):
        copies = []
        if both or way > 0:
            src = 0 if step == 1 else 2 * (step - 1)
            copies.append(remote(buffer.at[src], buffer.at[min(2 * step, 7)], ahead))
        if both or way < 0:
            src = 0 if step == 1 else 2 * (step - 1) - 1
            copies.append(remote(buffer.at[src], buffer.at[2 * step - 1], behind))
        return copies

    for copy in y_tok:
        copy.wait_recv()
    r_tok = ring(tok, 1, True, 0)
    for copy in y_cot:
        copy.wait_recv()
    r_cot = ring(cot, 1, True, 0)

    s_gate.wait_recv()
    fold(1)
    s_up.wait_recv()
    fold(3)
    s_down.wait_recv()

    def multiply(g):
        a, b = GROUPS[g]
        n = b - a
        t = tok[a:b].reshape(n * 64, 512)
        gate_up = dot(t, w_high[...], NT) + dot(t, w_low[...], NT)
        back = dot(cot[a:b].reshape(n * 64, 512), wd[...], NT)
        wide = t.astype(F32)
        back = put(back, 2 * UNITS, *pair(jnp.sum(wide * wide, axis=1, keepdims=True)))
        gate_up = gate_up.reshape(n, 4, 16, 4 * UNITS)
        back = back.reshape(n, 4, 16, 384)
        part[a:b, :, :, 0:640] = gate_up.astype(BF16)
        part[a:b, :, :, 640:1024] = back.astype(BF16)
        part_own[a:b, :, 0:640] = gate_up[:, 0]
        part_own[a:b, :, 640:1024] = back[:, 0]
        return [
            remote(part.at[pl.ds(a, n), k], rx.at[k - 1, pl.ds(a, n)], at(dx=k))
            for k in (1, 2, 3)
        ]

    def add_x(g, copies):
        a, b = GROUPS[g]
        n = b - a
        for copy in copies:
            copy.wait_recv()
        total = part_own[a:b]
        for k in range(3):
            total = total + rx[k, a:b].astype(F32)
        part_own[a:b] = total
        total = total.reshape(n * 16, 1024)
        squares = total[:, 960:961] + total[:, 961:962]
        y_out[a:b, :, 0:640] = total[:, 0:640].astype(BF16).reshape(n, 16, 640)
        last = put(total[:, 640:1024], 320, *pair(squares))
        y_out[a:b, :, 640:1024] = last.astype(BF16).reshape(n, 16, 384)
        return remote(y_out.at[pl.ds(a, n)], y_in.at[pl.ds(a, n)], across)

    x_sent, y_sent = [], []
    x_sent.append(multiply(0))
    for step in (1, 2, 3, 4):
        for copy in r_tok:
            copy.wait_recv()
        if step < 4:
            r_tok = ring(tok, step + 1, step < 3, -1)
        for copy in r_cot:
            copy.wait_recv()
        if step < 4:
            r_cot = ring(cot, step + 1, step < 3, 1)
        x_sent.append(multiply(step))
        y_sent.append(add_x(step - 1, x_sent[step - 1]))
    y_sent.append(add_x(4, x_sent[4]))

    def pointwise(g):
        a, b = GROUPS[g]
        n = b - a
        y_sent[g].wait_recv()
        total = (part_own[a:b] + y_in[a:b].astype(F32)).reshape(n * 16, 1024)
        squares = total[:, 960:961] + total[:, 961:962]
        inv_rms = lax.rsqrt(squares / D + EPSILON)
        gate_value = total[:, 0:320] * inv_rms
        up_value = total[:, 320:640] * inv_rms
        last = total[:, 640:1024]
        back = last[:, 0:320]
        activated, slope = gelu_parts(gate_value)
        grad_gate = (back * up_value * slope).astype(BF16)
        grad_up = (back * activated).astype(BF16)
        along = jnp.sum(
            grad_gate.astype(F32) * gate_value + grad_up.astype(F32) * up_value,
            axis=1,
            keepdims=True,
        )
        hid[a:b, 0, :, 0:640] = jnp.concatenate([grad_gate, grad_up], axis=1).reshape(n, 16, 640)
        hidden = jnp.concatenate([activated * up_value, jnp.zeros((n * 16, 64), F32)], axis=1)
        hidden = put(hidden, 320, *pair(along), *pair(inv_rms))
        hid[a:b, 0, :, 640:1024] = hidden.astype(BF16).reshape(n, 16, 384)
        return [
            remote(hid.at[pl.ds(a, n), 0], hid.at[pl.ds(a, n), 4 - k], at(dx=k))
            for k in (1, 2, 3)
        ]

    h_sent = {g: pointwise(g) for g in (0, 1, 4, 3, 2)}

    def inverse(block):
        return block[:, 962:963].astype(F32) + block[:, 963:964].astype(F32)

    def terms(g, gain_sum):
        a, b = GROUPS[g]
        n = b - a
        for copy in h_sent[g]:
            copy.wait_recv()
        block = hid[a:b].reshape(n * 64, 1024)
        branch_part[a:b] = dot(block[:, 640:1024], wd[...]).reshape(n, 64, 512)
        grad = dot(block[:, 0:640], w[...])
        scaled = tok[a:b].reshape(n * 64, 512).astype(F32) * inverse(block)
        normed[a:b] = (scaled * gain_v[...]).astype(BF16).reshape(n, 64, 512)
        gain_sum = gain_sum + jnp.sum(grad * scaled, axis=0, keepdims=True)
        gn_part[a:b, :, 0:512] = grad.reshape(n, 64, 512)
        along = block[:, 960:961].astype(F32) + block[:, 961:962].astype(F32)
        extra = put(jnp.zeros((n * 64, 128), F32), 0, along)
        gn_part[a:b, :, 512:640] = extra.reshape(n, 64, 128)
        return gain_sum

    def rounded(total):
        along = total[:, 512:513] + total[:, 513:514]
        return jnp.concatenate(
            [total[:, 0:512].astype(BF16), put(total[:, 512:640], 0, *pair(along)).astype(BF16)],
            axis=1,
        )

    gain_sum = jnp.zeros((1, 512), F32)
    arrived_b, arrived_g = {}, {}

    def pass_on(step):
        distance = 5 - step
        for way in (0, 1):
            slot = min(2 * distance - 1 + way, 7)
            there = (ahead, behind)[way]
            if step > 1 or way == 0:
                total = branch_part[slot]
                if (step - 1, way) in arrived_b:
                    arrived_b[step - 1, way].wait_recv()
                    total = total + ring_b[step - 2, way].astype(F32)
                ring_b_out[step - 1, way] = total.astype(BF16)
                arrived_b[step, way] = remote(
                    ring_b_out.at[step - 1, way], ring_b.at[step - 1, way], there
                )
        for way in (0, 1):
            slot = min(2 * distance - 1 + way, 7)
            there = (ahead, behind)[way]
            if step > 1 or way == 1:
                total = gn_part[slot]
                if (step - 1, way) in arrived_g:
                    arrived_g[step - 1, way].wait_recv()
                    total = total + ring_g[step - 2, way].astype(F32)
                ring_g_out[step - 1, way] = rounded(total)
                arrived_g[step, way] = remote(
                    ring_g_out.at[step - 1, way], ring_g.at[step - 1, way], there
                )

    gain_sum = terms(4, gain_sum)
    pass_on(1)
    gain_sum = terms(0, gain_sum)
    gain_sum = terms(1, gain_sum)
    gain_sum = terms(3, gain_sum)
    pass_on(2)
    gain_sum = terms(2, gain_sum)
    dgain[...] = jnp.broadcast_to(gain_sum, (8, 512))
    z_gain = [remote(dgain, dgain_in.at[k - 1], at(dz=k)) for k in range(1, 8)]

    every = hid[...].reshape(512, 1024)
    dw[...] = dot(every[:, 0:640], normed[...].reshape(512, 512), TN)
    dd[...] = dot(every[:, 640:1024], cot[...].reshape(512, 512), TN)
    w_sent = [
        remote(dw.at[pl.ds(UNITS, UNITS)], dw_in.at[0], sibling),
        remote(dw.at[pl.ds(3 * UNITS, UNITS)], dw_in.at[1], sibling),
        remote(dd.at[pl.ds(UNITS, UNITS)], dw_in.at[2], sibling),
    ]
    pass_on(3)

    for i, (grad, row, out) in enumerate(
        ((dw, 0, dgate_hbm), (dw, 2 * UNITS, dup_hbm), (dd, 0, ddown_hbm))
    ):
        w_sent[i].wait_recv()
        rows = pl.ds(row, UNITS)
        grad[rows] = grad[rows] + dw_in[i]
        bring(grad.at[rows], out)
    pass_on(4)

    for copy in z_gain:
        copy.wait_recv()
    total = dgain[...]
    for k in range(7):
        total = total + dgain_in[k]
    dgain_y[...] = total
    g_y = [remote(dgain_y, dgain_y_in.at[k - 1], at(dyl=k)) for k in (1, 2, 3)]

    arrived_b[4, 0].wait_recv()
    arrived_b[4, 1].wait_recv()
    total = branch_part[0] + ring_b[3, 0].astype(F32) + ring_b[3, 1].astype(F32)
    last_b[...] = total.reshape(4, 16, 512)
    last_b_out[...] = total.astype(BF16).reshape(4, 16, 512)
    y_b = [remote(last_b_out.at[piece(k)], last_b_in.at[k - 1], at(dyl=k)) for k in (1, 2, 3)]
    arrived_g[4, 0].wait_recv()
    arrived_g[4, 1].wait_recv()
    total = gn_part[0] + ring_g[3, 0].astype(F32) + ring_g[3, 1].astype(F32)
    last_g[...] = total.reshape(4, 16, 640)
    last_g_out[...] = rounded(total).reshape(4, 16, 640)
    y_g = [remote(last_g_out.at[piece(k)], last_g_in.at[k - 1], at(dyl=k)) for k in (1, 2, 3)]

    for copy in g_y:
        copy.wait_recv()
    total = dgain_y[...]
    for k in range(3):
        total = total + dgain_y_in[k]
    dgain_c[...] = total
    g_c = remote(dgain_c, dgain_c_in, sibling)

    for copy in y_b:
        copy.wait_recv()
    total = last_b[mine]
    for k in range(3):
        total = total + last_b_in[k].astype(F32)
    o_branch[...] = total.astype(BF16)
    bring(o_branch, branch_hbm)

    g_c.wait_recv()
    o_dgain[...] = (dgain_c[...] + dgain_c_in[...])[0:1]
    bring(o_dgain, dgain_hbm)

    inv_rms = inverse(hid[0, mine])
    scaled = own_tok[...].astype(F32) * inv_rms
    for copy in y_g:
        copy.wait_recv()
    total = last_g[mine]
    for k in range(3):
        total = total + last_g_in[k].astype(F32)
    row_mean = (total[:, 512:513] + total[:, 513:514]) / D
    o_gtok[...] = (inv_rms * (total[:, 0:512] * gain_v[...] - scaled * row_mean)).astype(BF16)
    bring(o_gtok, gtok_hbm)

    for copy in remote.all:
        copy.wait_send()
    for copy in local[7:]:
        copy.wait()


def hand_over(*refs):
    ins, outs, held = refs[:6], refs[6:12], refs[12:18]
    in_sem, out_sem = refs[18:]
    come = [pltpu.make_async_copy(a, b, in_sem.at[i]) for i, (a, b) in enumerate(zip(ins, held))]
    go = [pltpu.make_async_copy(a, b, out_sem.at[i]) for i, (a, b) in enumerate(zip(held, outs))]
    for copy in come:
        copy.start()
    for one, other in zip(come, go):
        one.wait()
        other.start()
    for copy in go:
        copy.wait()


def on_device(tokens, cotangent, norm_gain, gate_weight, up_weight, down_weight):
    vmem, dma = pltpu.VMEM, pltpu.SemaphoreType.DMA
    grad = jax.ShapeDtypeStruct((UNITS, 512), F32)
    shapes = (
        jax.ShapeDtypeStruct((16, 512), BF16),
        jax.ShapeDtypeStruct((16, 512), BF16),
        grad,
        grad,
        grad,
        jax.ShapeDtypeStruct((1, 512), F32),
    )
    outs = pl.pallas_call(
        kernel,
        out_shape=shapes,
        in_specs=[pl.BlockSpec(memory_space=pltpu.HBM)] * 6,
        out_specs=[pl.BlockSpec(memory_space=pltpu.HBM)] * 6,
        scratch_shapes=[
            vmem((16, 512), BF16),
            vmem((1, 512), F32),
            vmem((8, 4, 16, 512), BF16),
            vmem((8, 4, 16, 512), BF16),
            vmem((4 * UNITS, 512), BF16),
            vmem((4 * UNITS, 512), BF16),
            vmem((4 * UNITS, 512), BF16),
            vmem((384, 512), BF16),
            vmem((8, 4, 16, 1024), BF16),
            vmem((8, 16, 1024), F32),
            vmem((3, 8, 16, 1024), BF16),
            vmem((8, 16, 1024), BF16),
            vmem((8, 16, 1024), BF16),
            vmem((8, 4, 16, 1024), BF16),
            vmem((8, 64, 512), BF16),
            vmem((8, 64, 512), F32),
            vmem((8, 64, 640), F32),
            vmem((4, 2, 64, 512), BF16),
            vmem((4, 2, 64, 640), BF16),
            vmem((4, 2, 64, 512), BF16),
            vmem((4, 2, 64, 640), BF16),
            vmem((4, 16, 512), F32),
            vmem((4, 16, 640), F32),
            vmem((4, 16, 512), BF16),
            vmem((4, 16, 640), BF16),
            vmem((3, 16, 512), BF16),
            vmem((3, 16, 640), BF16),
            vmem((4 * UNITS, 512), F32),
            vmem((384, 512), F32),
            vmem((3, UNITS, 512), F32),
            vmem((8, 512), F32),
            vmem((7, 8, 512), F32),
            vmem((8, 512), F32),
            vmem((3, 8, 512), F32),
            vmem((8, 512), F32),
            vmem((8, 512), F32),
            vmem((16, 512), BF16),
            vmem((16, 512), BF16),
            vmem((1, 512), F32),
            dma((N_COPIES,)),
            dma((N_COPIES,)),
            dma((16,)),
        ],
        compiler_params=pltpu.CompilerParams(
            collective_id=0, has_side_effects=True, vmem_limit_bytes=63 * 1024 * 1024
        ),
        cost_estimate=pl.CostEstimate(flops=1_600_000_000, bytes_accessed=1_600_000, transcendentals=50_000),
    )(tokens, cotangent, norm_gain.reshape(1, 512), gate_weight, up_weight, down_weight)
    outs = pl.pallas_call(
        hand_over,
        out_shape=shapes,
        in_specs=[pl.BlockSpec(memory_space=pltpu.HBM)] * 6,
        out_specs=[pl.BlockSpec(memory_space=pltpu.HBM)] * 6,
        scratch_shapes=[*(vmem(a.shape, a.dtype) for a in shapes), dma((6,)), dma((6,))],
        compiler_params=pltpu.CompilerParams(vmem_limit_bytes=63 * 1024 * 1024),
    )(*outs)
    return (*outs[:5], outs[5].reshape(512))


def solution(mesh):
    split = P("dp", "node")
    return jax.shard_map(
        on_device,
        mesh=mesh,
        in_specs=(split, split, P("node"), split, split, split),
        out_specs=(split, split, split, split, split, P("node")),
        check_vma=False,
    )
```

```python
import functools
import math

import jax
import jax.numpy as jnp
from jax import lax
from jax.experimental import pallas as pl
from jax.experimental.pallas import tpu as pltpu
from jax.sharding import PartitionSpec as P

D = 4096
EPSILON = 1e-06
GELU_SCALE = math.sqrt(2.0 / math.pi)
MESH = pl.DeviceIdType.MESH
F32 = jnp.float32
BF16 = jnp.bfloat16

GROUPS = ((0, 1), (1, 3), (3, 5), (5, 7), (7, 8))
UNITS = 160
NT = (((1,), (1,)), ((), ()))
TN = (((0,), (0,)), ((), ()))


def dot(a, b, dims=None):
    if dims is None:
        return jnp.dot(a, b, preferred_element_type=F32)
    return lax.dot_general(a, b, dims, preferred_element_type=F32)


def gelu_parts(value):
    inner = GELU_SCALE * (value + 0.044715 * value * value * value)
    tanh_inner = jnp.tanh(inner)
    activated = 0.5 * value * (1.0 + tanh_inner)
    slope = 0.5 * (1.0 + tanh_inner) + 0.5 * value * (
        1.0 - tanh_inner * tanh_inner
    ) * GELU_SCALE * (1.0 + 3.0 * 0.044715 * value * value)
    return (activated, slope)


def pair(value):
    high = value.astype(BF16).astype(F32)
    return high, (value - high).astype(BF16).astype(F32)


def put(wide, lane, *values):
    at = lax.broadcasted_iota(jnp.int32, wide.shape, 1)
    for i, value in enumerate(values):
        wide = jnp.where(at == lane + i, value, wide)
    return wide


class Copies:
    def __init__(self, send_sem, recv_sem):
        self.send_sem, self.recv_sem, self.count, self.all = send_sem, recv_sem, 0, []

    def __call__(self, src, dst, device):
        i = self.count
        self.count += 1
        copy = pltpu.make_async_remote_copy(
            src_ref=src,
            dst_ref=dst,
            send_sem=self.send_sem.at[i],
            recv_sem=self.recv_sem.at[i],
            device_id=device,
            device_id_type=MESH,
        )
        copy.start()
        self.all.append(copy)
        return copy


N_COPIES = 128


def kernel(
    tok_hbm, cot_hbm, gain_hbm, gate_hbm, up_hbm, down_hbm,
    branch_hbm, gtok_hbm, dgate_hbm, dup_hbm, ddown_hbm, dgain_hbm,
    own_tok, gain_v, tok, cot, w, w_high, w_low, wd, part, part_own, rx, y_out, y_in, hid,
    normed, branch_part, gn_part, sums_in, sums_out,
    last_b, last_g, last_b_out, last_g_out, last_b_in, last_g_in,
    dw, dd, dw_in, dgain, dgain_in, dgain_y, dgain_y_in, dgain_c, dgain_c_in,
    o_branch, o_gtok, o_dgain,
    send_sem, recv_sem, local_sem,
):
    dp, node = lax.axis_index("dp"), lax.axis_index("node")
    x, yh = node // 2, node % 2
    yl, z, c = dp // 16, (dp // 2) % 8, dp % 2

    def at(dx=0, dyh=0, dyl=0, dz=0, dc=0):
        return (
            lax.rem(yl + dyl, 4) * 16 + lax.rem(z + dz, 8) * 2 + lax.rem(c + dc, 2),
            lax.rem(x + dx, 4) * 2 + lax.rem(yh + dyh, 2),
        )

    sibling, across = at(dc=1), at(dyh=1)
    ahead, behind = at(dz=1), at(dz=7)

    barrier = pltpu.get_barrier_semaphore()
    partners = [across, *(at(dz=k) for k in (4, 3, 5, 2, 6, 1, 7))]
    partners += [at(dyl=k) for k in (3, 2, 1)]
    partners += [at(dx=k) for k in (2, 1, 3)]
    partners += [sibling]
    for device in partners:
        pl.semaphore_signal(barrier, 1, device_id=device, device_id_type=MESH)

    def piece(k):
        return lax.rem(k - x + 8, 4)

    local = []

    def bring(src, dst):
        copy = pltpu.make_async_copy(src, dst, local_sem.at[len(local)])
        copy.start()
        local.append(copy)
        return copy

    mine = piece(0)
    b_tok = bring(tok_hbm, tok.at[0, mine])
    b_cot = bring(cot_hbm, cot.at[0, mine])
    b_own = bring(tok_hbm, own_tok)
    b_gain = bring(gain_hbm, gain_v)
    b_gate = bring(gate_hbm, w.at[pl.ds(0, UNITS)])
    b_up = bring(up_hbm, w.at[pl.ds(2 * UNITS, UNITS)])
    b_down = bring(down_hbm, wd.at[pl.ds(0, UNITS)])

    wd[pl.ds(2 * UNITS, 64)] = jnp.zeros((64, 512), BF16)
    pl.semaphore_wait(barrier, len(partners))

    remote = Copies(send_sem, recv_sem)

    y_tok = [remote(tok_hbm, tok.at[0, piece(4 - k)], at(dyl=k)) for k in (1, 2, 3)]
    y_cot = [remote(cot_hbm, cot.at[0, piece(4 - k)], at(dyl=k)) for k in (1, 2, 3)]
    s_gate = remote(gate_hbm, w.at[pl.ds(UNITS, UNITS)], sibling)
    s_up = remote(up_hbm, w.at[pl.ds(3 * UNITS, UNITS)], sibling)
    s_down = remote(down_hbm, wd.at[pl.ds(UNITS, UNITS)], sibling)

    def fold(block):
        rows = pl.ds(block * UNITS, UNITS)
        high, low = pair(w[rows].astype(F32) * gain_v[...])
        w_high[rows] = high.astype(BF16)
        w_low[rows] = low.astype(BF16)

    b_gain.wait()
    b_gate.wait()
    fold(0)
    b_up.wait()
    fold(2)
    b_tok.wait()
    b_cot.wait()
    b_down.wait()
    b_own.wait()

    def ring(buffer, step, way, arrived):
        copies = []
        for half in (0, 1):
            rows = pl.ds(2 * half, 2)
            for copy in arrived[half * len(arrived) // 2 : (half + 1) * len(arrived) // 2]:
                copy.wait_recv()
            if step < 5 and (step < 4 or way > 0):
                src = 0 if step == 1 else 2 * (step - 1)
                dst = min(2 * step, 7)
                copies.append(remote(buffer.at[src, rows], buffer.at[dst, rows], ahead))
            if step < 5 and (step < 4 or way < 0):
                src = 0 if step == 1 else 2 * (step - 1) - 1
                dst = 2 * step - 1
                copies.append(remote(buffer.at[src, rows], buffer.at[dst, rows], behind))
        return copies

    for copy in y_tok:
        copy.wait_recv()
    r_tok = ring(tok, 1, -1, [])
    for copy in y_cot:
        copy.wait_recv()
    r_cot = ring(cot, 1, 1, [])

    s_gate.wait_recv()
    fold(1)
    s_up.wait_recv()
    fold(3)
    s_down.wait_recv()

    def multiply(g):
        a, b = GROUPS[g]
        n = b - a
        t = tok[a:b].reshape(n * 64, 512)
        gate_up = dot(t, w_high[...], NT) + dot(t, w_low[...], NT)
        back = dot(cot[a:b].reshape(n * 64, 512), wd[...], NT)
        wide = t.astype(F32)
        back = put(back, 2 * UNITS, *pair(jnp.sum(wide * wide, axis=1, keepdims=True)))
        gate_up = gate_up.reshape(n, 4, 16, 4 * UNITS)
        back = back.reshape(n, 4, 16, 384)
        part[a:b, :, :, 0:640] = gate_up.astype(BF16)
        part[a:b, :, :, 640:1024] = back.astype(BF16)
        part_own[a:b, :, 0:640] = gate_up[:, 0]
        part_own[a:b, :, 640:1024] = back[:, 0]
        return [
            remote(part.at[pl.ds(a, n), k], rx.at[k - 1, pl.ds(a, n)], at(dx=k))
            for k in (1, 2, 3)
        ]

    def add_x(g, copies):
        a, b = GROUPS[g]
        n = b - a
        for copy in copies:
            copy.wait_recv()
        total = part_own[a:b]
        for k in range(3):
            total = total + rx[k, a:b].astype(F32)
        part_own[a:b] = total
        total = total.reshape(n * 16, 1024)
        squares = total[:, 960:961] + total[:, 961:962]
        y_out[a:b, :, 0:640] = total[:, 0:640].astype(BF16).reshape(n, 16, 640)
        last = put(total[:, 640:1024], 320, *pair(squares))
        y_out[a:b, :, 640:1024] = last.astype(BF16).reshape(n, 16, 384)
        return remote(y_out.at[pl.ds(a, n)], y_in.at[pl.ds(a, n)], across)

    x_sent, y_sent = [], []
    x_sent.append(multiply(0))
    for step in (1, 2, 3, 4):
        r_tok = ring(tok, step + 1, -1, r_tok)
        r_cot = ring(cot, step + 1, 1, r_cot)
        x_sent.append(multiply(step))
        if step > 1:
            y_sent.append(add_x(step - 2, x_sent[step - 2]))
    y_sent.append(add_x(3, x_sent[3]))

    def pointwise(g):
        a, b = GROUPS[g]
        n = b - a
        y_sent[g].wait_recv()
        total = (part_own[a:b] + y_in[a:b].astype(F32)).reshape(n * 16, 1024)
        squares = total[:, 960:961] + total[:, 961:962]
        inv_rms = lax.rsqrt(squares / D + EPSILON)
        gate_value = total[:, 0:320] * inv_rms
        up_value = total[:, 320:640] * inv_rms
        last = total[:, 640:1024]
        back = last[:, 0:320]
        activated, slope = gelu_parts(gate_value)
        grad_gate = (back * up_value * slope).astype(BF16)
        grad_up = (back * activated).astype(BF16)
        along = jnp.sum(
            grad_gate.astype(F32) * gate_value + grad_up.astype(F32) * up_value,
            axis=1,
            keepdims=True,
        )
        hid[a:b, 0, :, 0:640] = jnp.concatenate([grad_gate, grad_up], axis=1).reshape(n, 16, 640)
        hidden = jnp.concatenate([activated * up_value, jnp.zeros((n * 16, 64), F32)], axis=1)
        hidden = put(hidden, 320, *pair(along), *pair(inv_rms))
        hid[a:b, 0, :, 640:1024] = hidden.astype(BF16).reshape(n, 16, 384)
        return [
            remote(hid.at[pl.ds(a, n), 0], hid.at[pl.ds(a, n), 4 - k], at(dx=k))
            for k in (1, 2, 3)
        ]

    h_sent = {0: pointwise(0)}
    y_sent.append(add_x(4, x_sent[4]))
    for g in (1, 4, 3, 2):
        h_sent[g] = pointwise(g)

    def inverse(block):
        return block[:, 962:963].astype(F32) + block[:, 963:964].astype(F32)

    def terms(g, sums):
        a, b = GROUPS[g]
        n = b - a
        for copy in h_sent[g]:
            copy.wait_recv()
        block = hid[a:b].reshape(n * 64, 1024)
        branch_part[a:b] = dot(block[:, 640:1024], wd[...]).reshape(n, 64, 512)
        grad = dot(block[:, 0:640], w[...])
        scaled = tok[a:b].reshape(n * 64, 512).astype(F32) * inverse(block)
        normed[a:b] = (scaled * gain_v[...]).astype(BF16).reshape(n, 64, 512)
        gn_part[a:b] = grad.reshape(n, 64, 512)
        along = block[:, 960:961].astype(F32) + block[:, 961:962].astype(F32)
        row = lax.broadcasted_iota(jnp.int32, (n * 64, 512), 0)
        lane = lax.broadcasted_iota(jnp.int32, (n * 64, 512), 1)
        along = jnp.where(lane == row + a * 64, along, 0.0)
        return (
            sums[0] + jnp.sum(grad * scaled, axis=0, keepdims=True),
            sums[1] + jnp.sum(along, axis=0, keepdims=True),
        )

    def eight_rows(ref, first, second):
        for i in range(4):
            lanes = slice(i * 128, (i + 1) * 128)
            ref[i : i + 1] = first[:, lanes]
            ref[4 + i : 5 + i] = second[:, lanes]

    sums = (jnp.zeros((1, 512), F32), jnp.zeros((1, 512), F32))
    streams = [(branch_part, 0), (branch_part, 1), (gn_part, 0), (gn_part, 1)]
    arrived = {}

    def so_far(slot, stream, *known):
        source, half = streams[stream]
        total = source[slot, :, half * 256 : (half + 1) * 256]
        for step, way in known:
            if (step, way, stream) in arrived:
                arrived[step, way, stream].wait_recv()
                total = total + sums_in[step - 1, way, stream].astype(F32)
        return total

    def pass_on(step):
        for stream in range(4):
            for way in (0, 1):
                if step == 1 and way != stream // 2:
                    continue
                slot = min(2 * (5 - step) - 1 + way, 7)
                sums_out[step - 1, way, stream] = so_far(slot, stream, (step - 1, way)).astype(BF16)
                arrived[step, way, stream] = remote(
                    sums_out.at[step - 1, way, stream],
                    sums_in.at[step - 1, way, stream],
                    (ahead, behind)[way],
                )

    sums = terms(4, sums)
    pass_on(1)
    sums = terms(0, sums)
    sums = terms(1, sums)
    sums = terms(3, sums)
    pass_on(2)
    sums = terms(2, sums)
    eight_rows(dgain, *sums)
    z_gain = [remote(dgain, dgain_in.at[k - 1], at(dz=k)) for k in range(1, 8)]

    every = hid[...].reshape(512, 1024)
    dw[...] = dot(every[:, 0:640], normed[...].reshape(512, 512), TN)
    dd[...] = dot(every[:, 640:1024], cot[...].reshape(512, 512), TN)
    w_sent = [
        remote(dw.at[pl.ds(UNITS, UNITS)], dw_in.at[0], sibling),
        remote(dw.at[pl.ds(3 * UNITS, UNITS)], dw_in.at[1], sibling),
        remote(dd.at[pl.ds(UNITS, UNITS)], dw_in.at[2], sibling),
    ]
    pass_on(3)

    for i, (grad, row, out) in enumerate(
        ((dw, 0, dgate_hbm), (dw, 2 * UNITS, dup_hbm), (dd, 0, ddown_hbm))
    ):
        w_sent[i].wait_recv()
        rows = pl.ds(row, UNITS)
        grad[rows] = grad[rows] + dw_in[i]
        bring(grad.at[rows], out)
    pass_on(4)

    for copy in z_gain:
        copy.wait_recv()
    gain_total, along = dgain[0:4], dgain[4:5]
    low = lax.broadcasted_iota(jnp.int32, (1, 128), 1) < 64
    for k in range(1, 8):
        slot = 2 * k - 1 if k < 5 else 2 * (8 - k)
        gain_total = gain_total + dgain_in[k - 1, 0:4]
        row = dgain_in[k - 1, 4 + slot // 2 : 5 + slot // 2]
        along = along + (pltpu.roll(row, 64, 1) if slot % 2 else row)
    dgain_y[0:4] = gain_total
    dgain_y[4:8] = jnp.broadcast_to(jnp.where(low, along, 0.0), (4, 128))
    g_y = [remote(dgain_y, dgain_y_in.at[k - 1], at(dyl=k)) for k in (1, 2, 3)]

    def finish(array, total, out, landing):
        for half in (0, 1):
            lanes = slice(half * 256, (half + 1) * 256)
            part_sum = so_far(0, 2 * array + half, (4, 0), (4, 1)).reshape(4, 16, 256)
            total[:, :, lanes] = part_sum
            out[:, :, lanes] = part_sum.astype(BF16)
        return [remote(out.at[piece(k)], landing.at[k - 1], at(dyl=k)) for k in (1, 2, 3)]

    y_b = finish(0, last_b, last_b_out, last_b_in)
    y_g = finish(1, last_g, last_g_out, last_g_in)

    for copy in g_y:
        copy.wait_recv()
    total = dgain_y[...]
    for k in range(3):
        total = total + dgain_y_in[k]
    dgain_c[...] = total
    row = lax.broadcasted_iota(jnp.int32, (16, 128), 0)
    lane = lax.broadcasted_iota(jnp.int32, (16, 128), 1)
    along = jnp.where(lane == row + mine * 16, dgain_y[4:5], 0.0)
    for k in (1, 2, 3):
        along = along + jnp.where(lane == row + piece(k) * 16, dgain_y_in[k - 1, 4:5], 0.0)
    row_mean = jnp.sum(along, axis=1, keepdims=True) / D
    g_c = remote(dgain_c, dgain_c_in, sibling)

    for copy in y_b:
        copy.wait_recv()
    total = last_b[mine]
    for k in range(3):
        total = total + last_b_in[k].astype(F32)
    o_branch[...] = total.astype(BF16)
    bring(o_branch, branch_hbm)

    g_c.wait_recv()
    o_dgain[...] = (dgain_c[...] + dgain_c_in[...])[0:4]
    bring(o_dgain, dgain_hbm)

    inv_rms = inverse(hid[0, mine])
    scaled = own_tok[...].astype(F32) * inv_rms
    for copy in y_g:
        copy.wait_recv()
    total = last_g[mine]
    for k in range(3):
        total = total + last_g_in[k].astype(F32)
    o_gtok[...] = (inv_rms * (total * gain_v[...] - scaled * row_mean)).astype(BF16)
    bring(o_gtok, gtok_hbm)

    for copy in remote.all:
        copy.wait_send()
    for copy in local[7:]:
        copy.wait()


def hand_over(*refs):
    ins, outs, held = refs[:6], refs[6:12], refs[12:18]
    in_sem, out_sem = refs[18:]
    come = [pltpu.make_async_copy(a, b, in_sem.at[i]) for i, (a, b) in enumerate(zip(ins, held))]
    go = [pltpu.make_async_copy(a, b, out_sem.at[i]) for i, (a, b) in enumerate(zip(held, outs))]
    for copy in come:
        copy.start()
    for one, other in zip(come, go):
        one.wait()
        other.start()
    for copy in go:
        copy.wait()


def on_device(tokens, cotangent, norm_gain, gate_weight, up_weight, down_weight):
    vmem, dma = pltpu.VMEM, pltpu.SemaphoreType.DMA
    grad = jax.ShapeDtypeStruct((UNITS, 512), F32)
    shapes = (
        jax.ShapeDtypeStruct((16, 512), BF16),
        jax.ShapeDtypeStruct((16, 512), BF16),
        grad,
        grad,
        grad,
        jax.ShapeDtypeStruct((4, 128), F32),
    )
    outs = pl.pallas_call(
        kernel,
        out_shape=shapes,
        in_specs=[pl.BlockSpec(memory_space=pltpu.HBM)] * 6,
        out_specs=[pl.BlockSpec(memory_space=pltpu.HBM)] * 6,
        scratch_shapes=[
            vmem((16, 512), BF16),
            vmem((1, 512), F32),
            vmem((8, 4, 16, 512), BF16),
            vmem((8, 4, 16, 512), BF16),
            vmem((4 * UNITS, 512), BF16),
            vmem((4 * UNITS, 512), BF16),
            vmem((4 * UNITS, 512), BF16),
            vmem((384, 512), BF16),
            vmem((8, 4, 16, 1024), BF16),
            vmem((8, 16, 1024), F32),
            vmem((3, 8, 16, 1024), BF16),
            vmem((8, 16, 1024), BF16),
            vmem((8, 16, 1024), BF16),
            vmem((8, 4, 16, 1024), BF16),
            vmem((8, 64, 512), BF16),
            vmem((8, 64, 512), F32),
            vmem((8, 64, 512), F32),
            vmem((4, 2, 4, 64, 256), BF16),
            vmem((4, 2, 4, 64, 256), BF16),
            vmem((4, 16, 512), F32),
            vmem((4, 16, 512), F32),
            vmem((4, 16, 512), BF16),
            vmem((4, 16, 512), BF16),
            vmem((3, 16, 512), BF16),
            vmem((3, 16, 512), BF16),
            vmem((4 * UNITS, 512), F32),
            vmem((384, 512), F32),
            vmem((3, UNITS, 512), F32),
            vmem((8, 128), F32),
            vmem((7, 8, 128), F32),
            vmem((8, 128), F32),
            vmem((3, 8, 128), F32),
            vmem((8, 128), F32),
            vmem((8, 128), F32),
            vmem((16, 512), BF16),
            vmem((16, 512), BF16),
            vmem((4, 128), F32),
            dma((N_COPIES,)),
            dma((N_COPIES,)),
            dma((16,)),
        ],
        compiler_params=pltpu.CompilerParams(
            collective_id=0, has_side_effects=True, vmem_limit_bytes=63 * 1024 * 1024
        ),
        cost_estimate=pl.CostEstimate(flops=1_600_000_000, bytes_accessed=1_600_000, transcendentals=50_000),
    )(tokens, cotangent, norm_gain.reshape(1, 512), gate_weight, up_weight, down_weight)
    outs = pl.pallas_call(
        hand_over,
        out_shape=shapes,
        in_specs=[pl.BlockSpec(memory_space=pltpu.HBM)] * 6,
        out_specs=[pl.BlockSpec(memory_space=pltpu.HBM)] * 6,
        scratch_shapes=[*(vmem(a.shape, a.dtype) for a in shapes), dma((6,)), dma((6,))],
        compiler_params=pltpu.CompilerParams(vmem_limit_bytes=63 * 1024 * 1024),
    )(*outs)
    return (*outs[:5], outs[5].reshape(512))


def solution(mesh):
    split = P("dp", "node")
    return jax.shard_map(
        on_device,
        mesh=mesh,
        in_specs=(split, split, P("node"), split, split, split),
        out_specs=(split, split, split, split, split, P("node")),
        check_vma=False,
    )
```

```python
import functools
import math

import jax
import jax.numpy as jnp
from jax import lax
from jax.experimental import pallas as pl
from jax.experimental.pallas import tpu as pltpu
from jax.sharding import PartitionSpec as P

D = 4096
EPSILON = 1e-06
GELU_SCALE = math.sqrt(2.0 / math.pi)
MESH = pl.DeviceIdType.MESH
F32 = jnp.float32
BF16 = jnp.bfloat16

GROUPS = ((0, 1), (1, 3), (3, 5), (5, 7), (7, 8))
UNITS = 160
NT = (((1,), (1,)), ((), ()))
TN = (((0,), (0,)), ((), ()))


def dot(a, b, dims=None):
    if dims is None:
        return jnp.dot(a, b, preferred_element_type=F32)
    return lax.dot_general(a, b, dims, preferred_element_type=F32)


def gelu_parts(value):
    inner = GELU_SCALE * (value + 0.044715 * value * value * value)
    tanh_inner = jnp.tanh(inner)
    activated = 0.5 * value * (1.0 + tanh_inner)
    slope = 0.5 * (1.0 + tanh_inner) + 0.5 * value * (
        1.0 - tanh_inner * tanh_inner
    ) * GELU_SCALE * (1.0 + 3.0 * 0.044715 * value * value)
    return (activated, slope)


def pair(value):
    high = value.astype(BF16).astype(F32)
    return high, (value - high).astype(BF16).astype(F32)


def put(wide, lane, *values):
    at = lax.broadcasted_iota(jnp.int32, wide.shape, 1)
    for i, value in enumerate(values):
        wide = jnp.where(at == lane + i, value, wide)
    return wide


class Copies:
    def __init__(self, send_sem, recv_sem):
        self.send_sem, self.recv_sem, self.count, self.all = send_sem, recv_sem, 0, []

    def __call__(self, src, dst, device):
        i = self.count
        self.count += 1
        copy = pltpu.make_async_remote_copy(
            src_ref=src,
            dst_ref=dst,
            send_sem=self.send_sem.at[i],
            recv_sem=self.recv_sem.at[i],
            device_id=device,
            device_id_type=MESH,
        )
        copy.start()
        self.all.append(copy)
        return copy


N_COPIES = 128


def kernel(
    tok_hbm, cot_hbm, gain_hbm, gate_hbm, up_hbm, down_hbm,
    branch_hbm, gtok_hbm, dgate_hbm, dup_hbm, ddown_hbm, dgain_hbm,
    own_tok, gain_v, tok, cot, w, w_high, w_low, wd, part, part_own, rx, y_out, y_in, hid,
    normed, branch_part, gn_part, sums_in, sums_out,
    last_b, last_g, last_b_out, last_g_out, last_b_in, last_g_in,
    dw, dd, dw_in, dgain, dgain_in, dgain_y, dgain_y_in, dgain_c, dgain_c_in,
    o_branch, o_gtok, o_dgain,
    send_sem, recv_sem, local_sem,
):
    dp, node = lax.axis_index("dp"), lax.axis_index("node")
    x, yh = node // 2, node % 2
    yl, z, c = dp // 16, (dp // 2) % 8, dp % 2

    def at(dx=0, dyh=0, dyl=0, dz=0, dc=0):
        return (
            lax.rem(yl + dyl, 4) * 16 + lax.rem(z + dz, 8) * 2 + lax.rem(c + dc, 2),
            lax.rem(x + dx, 4) * 2 + lax.rem(yh + dyh, 2),
        )

    sibling, across = at(dc=1), at(dyh=1)
    ahead, behind = at(dz=1), at(dz=7)

    barrier = pltpu.get_barrier_semaphore()
    partners = [across, *(at(dz=k) for k in (4, 3, 5, 2, 6, 1, 7))]
    partners += [at(dyl=k) for k in (3, 2, 1)]
    partners += [at(dx=k) for k in (2, 1, 3)]
    partners += [sibling]
    for device in partners:
        pl.semaphore_signal(barrier, 1, device_id=device, device_id_type=MESH)

    def piece(k):
        return lax.rem(k - x + 8, 4)

    local = []

    def bring(src, dst):
        copy = pltpu.make_async_copy(src, dst, local_sem.at[len(local)])
        copy.start()
        local.append(copy)
        return copy

    mine = piece(0)
    b_tok = bring(tok_hbm, tok.at[0, mine])
    b_cot = bring(cot_hbm, cot.at[0, mine])
    b_own = bring(tok_hbm, own_tok)
    b_gain = bring(gain_hbm, gain_v)
    b_gate = bring(gate_hbm, w.at[pl.ds(0, UNITS)])
    b_up = bring(up_hbm, w.at[pl.ds(2 * UNITS, UNITS)])
    b_down = bring(down_hbm, wd.at[pl.ds(0, UNITS)])

    wd[pl.ds(2 * UNITS, 64)] = jnp.zeros((64, 512), BF16)
    pl.semaphore_wait(barrier, len(partners))

    remote = Copies(send_sem, recv_sem)

    y_tok = [remote(tok_hbm, tok.at[0, piece(4 - k)], at(dyl=k)) for k in (1, 2, 3)]
    y_cot = [remote(cot_hbm, cot.at[0, piece(4 - k)], at(dyl=k)) for k in (1, 2, 3)]
    s_gate = remote(gate_hbm, w.at[pl.ds(UNITS, UNITS)], sibling)
    s_up = remote(up_hbm, w.at[pl.ds(3 * UNITS, UNITS)], sibling)
    s_down = remote(down_hbm, wd.at[pl.ds(UNITS, UNITS)], sibling)

    def fold(block):
        rows = pl.ds(block * UNITS, UNITS)
        high, low = pair(w[rows].astype(F32) * gain_v[...])
        w_high[rows] = high.astype(BF16)
        w_low[rows] = low.astype(BF16)

    b_gain.wait()
    b_gate.wait()
    fold(0)
    b_up.wait()
    fold(2)
    b_tok.wait()
    b_cot.wait()
    b_down.wait()
    b_own.wait()

    def ring(buffer, step, way, arrived):
        copies = []
        for half in (0, 1):
            rows = pl.ds(2 * half, 2)
            for copy in arrived[half * len(arrived) // 2 : (half + 1) * len(arrived) // 2]:
                copy.wait_recv()
            if step < 5 and (step < 4 or way > 0):
                src = 0 if step == 1 else 2 * (step - 1)
                dst = min(2 * step, 7)
                copies.append(remote(buffer.at[src, rows], buffer.at[dst, rows], ahead))
            if step < 5 and (step < 4 or way < 0):
                src = 0 if step == 1 else 2 * (step - 1) - 1
                dst = 2 * step - 1
                copies.append(remote(buffer.at[src, rows], buffer.at[dst, rows], behind))
        return copies

    for copy in y_tok:
        copy.wait_recv()
    r_tok = ring(tok, 1, -1, [])
    for copy in y_cot:
        copy.wait_recv()
    r_cot = ring(cot, 1, 1, [])

    s_gate.wait_recv()
    fold(1)
    s_up.wait_recv()
    fold(3)
    s_down.wait_recv()

    def multiply(g):
        a, b = GROUPS[g]
        n = b - a
        t = tok[a:b].reshape(n * 64, 512)
        gate_up = dot(t, w_high[...], NT) + dot(t, w_low[...], NT)
        back = dot(cot[a:b].reshape(n * 64, 512), wd[...], NT)
        wide = t.astype(F32)
        back = put(back, 2 * UNITS, *pair(jnp.sum(wide * wide, axis=1, keepdims=True)))
        gate_up = gate_up.reshape(n, 4, 16, 4 * UNITS)
        back = back.reshape(n, 4, 16, 384)
        part[a:b, :, :, 0:640] = gate_up.astype(BF16)
        part[a:b, :, :, 640:1024] = back.astype(BF16)
        part_own[a:b, :, 0:640] = gate_up[:, 0]
        part_own[a:b, :, 640:1024] = back[:, 0]
        return [
            remote(part.at[pl.ds(a, n), k], rx.at[k - 1, pl.ds(a, n)], at(dx=k))
            for k in (1, 2, 3)
        ]

    def add_x(g, copies):
        a, b = GROUPS[g]
        n = b - a
        for copy in copies:
            copy.wait_recv()
        total = part_own[a:b]
        for k in range(3):
            total = total + rx[k, a:b].astype(F32)
        part_own[a:b] = total
        total = total.reshape(n * 16, 1024)
        squares = total[:, 960:961] + total[:, 961:962]
        y_out[a:b, :, 0:640] = total[:, 0:640].astype(BF16).reshape(n, 16, 640)
        last = put(total[:, 640:1024], 320, *pair(squares))
        y_out[a:b, :, 640:1024] = last.astype(BF16).reshape(n, 16, 384)
        return remote(y_out.at[pl.ds(a, n)], y_in.at[pl.ds(a, n)], across)

    x_sent, y_sent = [], []
    x_sent.append(multiply(0))
    for step in (1, 2, 3, 4):
        r_tok = ring(tok, step + 1, -1, r_tok)
        r_cot = ring(cot, step + 1, 1, r_cot)
        x_sent.append(multiply(step))
        if step > 1:
            y_sent.append(add_x(step - 2, x_sent[step - 2]))
    y_sent.append(add_x(3, x_sent[3]))

    def pointwise(g):
        a, b = GROUPS[g]
        n = b - a
        y_sent[g].wait_recv()
        total = (part_own[a:b] + y_in[a:b].astype(F32)).reshape(n * 16, 1024)
        squares = total[:, 960:961] + total[:, 961:962]
        inv_rms = lax.rsqrt(squares / D + EPSILON)
        gate_value = total[:, 0:320] * inv_rms
        up_value = total[:, 320:640] * inv_rms
        last = total[:, 640:1024]
        back = last[:, 0:320]
        activated, slope = gelu_parts(gate_value)
        grad_gate = (back * up_value * slope).astype(BF16)
        grad_up = (back * activated).astype(BF16)
        along = jnp.sum(
            grad_gate.astype(F32) * gate_value + grad_up.astype(F32) * up_value,
            axis=1,
            keepdims=True,
        )
        hid[a:b, 0, :, 0:640] = jnp.concatenate([grad_gate, grad_up], axis=1).reshape(n, 16, 640)
        hidden = jnp.concatenate([activated * up_value, jnp.zeros((n * 16, 64), F32)], axis=1)
        hidden = put(hidden, 320, *pair(along), *pair(inv_rms))
        hid[a:b, 0, :, 640:1024] = hidden.astype(BF16).reshape(n, 16, 384)
        return [
            remote(hid.at[pl.ds(a, n), 0], hid.at[pl.ds(a, n), 4 - k], at(dx=k))
            for k in (1, 2, 3)
        ]

    h_sent = {0: pointwise(0)}
    y_sent.append(add_x(4, x_sent[4]))
    for g in (1, 4, 3, 2):
        h_sent[g] = pointwise(g)

    def inverse(block):
        return block[:, 962:963].astype(F32) + block[:, 963:964].astype(F32)

    def terms(g, sums):
        a, b = GROUPS[g]
        n = b - a
        for copy in h_sent[g]:
            copy.wait_recv()
        block = hid[a:b].reshape(n * 64, 1024)
        branch_part[a:b] = dot(block[:, 640:1024], wd[...]).reshape(n, 64, 512)
        grad = dot(block[:, 0:640], w[...])
        scaled = tok[a:b].reshape(n * 64, 512).astype(F32) * inverse(block)
        normed[a:b] = (scaled * gain_v[...]).astype(BF16).reshape(n, 64, 512)
        gn_part[a:b] = grad.reshape(n, 64, 512)
        along = block[:, 960:961].astype(F32) + block[:, 961:962].astype(F32)
        row = lax.broadcasted_iota(jnp.int32, (n * 64, 512), 0)
        lane = lax.broadcasted_iota(jnp.int32, (n * 64, 512), 1)
        along = jnp.where(lane == row + a * 64, along, 0.0)
        return (
            sums[0] + jnp.sum(grad * scaled, axis=0, keepdims=True),
            sums[1] + jnp.sum(along, axis=0, keepdims=True),
        )

    def eight_rows(ref, first, second):
        for i in range(4):
            lanes = slice(i * 128, (i + 1) * 128)
            ref[i : i + 1] = first[:, lanes]
            ref[4 + i : 5 + i] = second[:, lanes]

    sums = (jnp.zeros((1, 512), F32), jnp.zeros((1, 512), F32))
    streams = [(branch_part, 0), (branch_part, 1), (gn_part, 0), (gn_part, 1)]
    arrived = {}

    def so_far(slot, stream, *known):
        source, half = streams[stream]
        total = source[slot, :, half * 256 : (half + 1) * 256]
        for step, way in known:
            if (step, way, stream) in arrived:
                arrived[step, way, stream].wait_recv()
                total = total + sums_in[step - 1, way, stream].astype(F32)
        return total

    def pass_on(step):
        for stream in range(4):
            for way in (0, 1):
                if step == 1 and way != stream // 2:
                    continue
                slot = min(2 * (5 - step) - 1 + way, 7)
                sums_out[step - 1, way, stream] = so_far(slot, stream, (step - 1, way)).astype(BF16)
                arrived[step, way, stream] = remote(
                    sums_out.at[step - 1, way, stream],
                    sums_in.at[step - 1, way, stream],
                    (ahead, behind)[way],
                )

    sums = terms(4, sums)
    pass_on(1)
    sums = terms(0, sums)
    sums = terms(1, sums)
    sums = terms(3, sums)
    pass_on(2)
    sums = terms(2, sums)
    eight_rows(dgain, *sums)
    z_gain = [remote(dgain, dgain_in.at[k - 1], at(dz=k)) for k in range(1, 8)]

    every = hid[...].reshape(512, 1024)
    dw[...] = dot(every[:, 0:640], normed[...].reshape(512, 512), TN)
    dd[...] = dot(every[:, 640:1024], cot[...].reshape(512, 512), TN)
    w_sent = [
        remote(dw.at[pl.ds(UNITS, UNITS)], dw_in.at[0], sibling),
        remote(dw.at[pl.ds(3 * UNITS, UNITS)], dw_in.at[1], sibling),
        remote(dd.at[pl.ds(UNITS, UNITS)], dw_in.at[2], sibling),
    ]
    pass_on(3)

    for i, (grad, row, out) in enumerate(
        ((dw, 0, dgate_hbm), (dw, 2 * UNITS, dup_hbm), (dd, 0, ddown_hbm))
    ):
        w_sent[i].wait_recv()
        rows = pl.ds(row, UNITS)
        grad[rows] = grad[rows] + dw_in[i]
        bring(grad.at[rows], out)
    pass_on(4)

    for copy in z_gain:
        copy.wait_recv()
    gain_total, along = dgain[0:4], dgain[4:5]
    low = lax.broadcasted_iota(jnp.int32, (1, 128), 1) < 64
    for k in range(1, 8):
        slot = 2 * k - 1 if k < 5 else 2 * (8 - k)
        gain_total = gain_total + dgain_in[k - 1, 0:4]
        row = dgain_in[k - 1, 4 + slot // 2 : 5 + slot // 2]
        along = along + (pltpu.roll(row, 64, 1) if slot % 2 else row)
    dgain_y[0:4] = gain_total
    dgain_y[4:8] = jnp.broadcast_to(jnp.where(low, along, 0.0), (4, 128))
    g_y = [remote(dgain_y, dgain_y_in.at[k - 1], at(dyl=k)) for k in (1, 2, 3)]

    def finish(array, total, out, landing):
        for half in (0, 1):
            lanes = slice(half * 256, (half + 1) * 256)
            part_sum = so_far(0, 2 * array + half, (4, 0), (4, 1)).reshape(4, 16, 256)
            total[:, :, lanes] = part_sum
            out[:, :, lanes] = part_sum.astype(BF16)
        return [remote(out.at[piece(k)], landing.at[k - 1], at(dyl=k)) for k in (1, 2, 3)]

    y_b = finish(0, last_b, last_b_out, last_b_in)
    y_g = finish(1, last_g, last_g_out, last_g_in)

    for copy in g_y:
        copy.wait_recv()
    total = dgain_y[...]
    for k in range(3):
        total = total + dgain_y_in[k]
    dgain_c[...] = total
    row = lax.broadcasted_iota(jnp.int32, (16, 128), 0)
    lane = lax.broadcasted_iota(jnp.int32, (16, 128), 1)
    along = jnp.where(lane == row + mine * 16, dgain_y[4:5], 0.0)
    for k in (1, 2, 3):
        along = along + jnp.where(lane == row + piece(k) * 16, dgain_y_in[k - 1, 4:5], 0.0)
    row_mean = jnp.sum(along, axis=1, keepdims=True) / D
    g_c = remote(dgain_c, dgain_c_in, sibling)

    for copy in y_b:
        copy.wait_recv()
    total = last_b[mine]
    for k in range(3):
        total = total + last_b_in[k].astype(F32)
    o_branch[...] = total.astype(BF16)
    bring(o_branch, branch_hbm)

    g_c.wait_recv()
    o_dgain[...] = (dgain_c[...] + dgain_c_in[...])[0:4]
    bring(o_dgain, dgain_hbm)

    inv_rms = inverse(hid[0, mine])
    scaled = own_tok[...].astype(F32) * inv_rms
    for copy in y_g:
        copy.wait_recv()
    total = last_g[mine]
    for k in range(3):
        total = total + last_g_in[k].astype(F32)
    o_gtok[...] = (inv_rms * (total * gain_v[...] - scaled * row_mean)).astype(BF16)
    bring(o_gtok, gtok_hbm)

    for copy in remote.all:
        copy.wait_send()
    for copy in local[7:]:
        copy.wait()


def hand_over(*refs):
    ins, outs, sem = refs[:6], refs[6:12], refs[12]
    copies = [pltpu.make_async_copy(a, b, sem.at[i]) for i, (a, b) in enumerate(zip(ins, outs))]
    for copy in copies:
        copy.start()
    for copy in copies:
        copy.wait()


def on_device(tokens, cotangent, norm_gain, gate_weight, up_weight, down_weight):
    vmem, dma = pltpu.VMEM, pltpu.SemaphoreType.DMA
    grad = jax.ShapeDtypeStruct((UNITS, 512), F32)
    shapes = (
        jax.ShapeDtypeStruct((16, 512), BF16),
        jax.ShapeDtypeStruct((16, 512), BF16),
        grad,
        grad,
        grad,
        jax.ShapeDtypeStruct((4, 128), F32),
    )
    outs = pl.pallas_call(
        kernel,
        out_shape=tuple(vmem(a.shape, a.dtype) for a in shapes),
        in_specs=[pl.BlockSpec(memory_space=pltpu.HBM)] * 6,
        out_specs=[pl.BlockSpec(memory_space=pl.ANY)] * 6,
        scratch_shapes=[
            vmem((16, 512), BF16),
            vmem((1, 512), F32),
            vmem((8, 4, 16, 512), BF16),
            vmem((8, 4, 16, 512), BF16),
            vmem((4 * UNITS, 512), BF16),
            vmem((4 * UNITS, 512), BF16),
            vmem((4 * UNITS, 512), BF16),
            vmem((384, 512), BF16),
            vmem((8, 4, 16, 1024), BF16),
            vmem((8, 16, 1024), F32),
            vmem((3, 8, 16, 1024), BF16),
            vmem((8, 16, 1024), BF16),
            vmem((8, 16, 1024), BF16),
            vmem((8, 4, 16, 1024), BF16),
            vmem((8, 64, 512), BF16),
            vmem((8, 64, 512), F32),
            vmem((8, 64, 512), F32),
            vmem((4, 2, 4, 64, 256), BF16),
            vmem((4, 2, 4, 64, 256), BF16),
            vmem((4, 16, 512), F32),
            vmem((4, 16, 512), F32),
            vmem((4, 16, 512), BF16),
            vmem((4, 16, 512), BF16),
            vmem((3, 16, 512), BF16),
            vmem((3, 16, 512), BF16),
            vmem((4 * UNITS, 512), F32),
            vmem((384, 512), F32),
            vmem((3, UNITS, 512), F32),
            vmem((8, 128), F32),
            vmem((7, 8, 128), F32),
            vmem((8, 128), F32),
            vmem((3, 8, 128), F32),
            vmem((8, 128), F32),
            vmem((8, 128), F32),
            vmem((16, 512), BF16),
            vmem((16, 512), BF16),
            vmem((4, 128), F32),
            dma((N_COPIES,)),
            dma((N_COPIES,)),
            dma((16,)),
        ],
        compiler_params=pltpu.CompilerParams(
            collective_id=0, has_side_effects=True, vmem_limit_bytes=60 * 1024 * 1024
        ),
        cost_estimate=pl.CostEstimate(flops=1_600_000_000, bytes_accessed=1_600_000, transcendentals=50_000),
    )(tokens, cotangent, norm_gain.reshape(1, 512), gate_weight, up_weight, down_weight)
    outs = pl.pallas_call(
        hand_over,
        out_shape=shapes,
        in_specs=[pl.BlockSpec(memory_space=pl.ANY)] * 6,
        out_specs=[pl.BlockSpec(memory_space=pltpu.HBM)] * 6,
        scratch_shapes=[dma((6,))],
        compiler_params=pltpu.CompilerParams(vmem_limit_bytes=2 * 1024 * 1024),
    )(*outs)
    return (*outs[:5], outs[5].reshape(512))


def solution(mesh):
    split = P("dp", "node")
    return jax.shard_map(
        on_device,
        mesh=mesh,
        in_specs=(split, split, P("node"), split, split, split),
        out_specs=(split, split, split, split, split, P("node")),
        check_vma=False,
    )
```
